32 devices in a mesh: groups: 2 (over x), series: 16 (over z, y, core).
Axes of the slice: x: 2, y: 2, z: 4, core: 2. Of those that a mesh axis runs over, the one named last changes fastest.
Arguments:
- series_data: bfloat16 [65536, 1024], P(('groups', 'series')), parts along dimension 0, may hold values from -90 to 90
- sketch_matrix: bfloat16 [2048, 256], P(('groups', 'series')), parts along dimension 0, may hold values from -0.1875 to 0.1875
Outputs:
- range_basis: bfloat16 [65536, 256], P(('groups', 'series')), parts along dimension 0
- coefficients: bfloat16 [2048, 256], P(('groups', 'series')), parts along dimension 0
The draws below stay inside these ranges and needn't reach their ends.
There are 2 independent parts, one for each index of `groups`. The reference program is written for one: setup_inputs(seed, part) draws one part's arguments, and reference() takes and returns one part's arrays. A program takes and returns all parts, laid end to end along the dimension named above; each array names one. Nothing has to cross between parts.
All inputs are finite; a program needn't handle non-finite values.
Results may differ from the reference program's by a relative error of at most 0.0054.
Values may be sent and summed in bfloat16 or wider, within the bound.
No kernel may reach another device: no remote copies, remote signals or barrier semaphores. Data moves between devices by JAX's collectives and lax.ppermute only.
A program may use at most 64 MiB of HBM per device.

```python
import math
import jax
import jax.numpy as jnp
from jax import lax

RANK = 256
TIME = 1024
ROWS = 32768


def draw_series_data(key, part):
    key = jax.random.fold_in(key, 11)
    keys = jax.random.split(key, 3)
    positions = jnp.arange(ROWS, dtype=jnp.float32) / ROWS - 0.5
    noise = jnp.clip(jax.random.normal(keys[0], (ROWS, TIME), jnp.float32), -6.0, 6.0)
    ramp = jnp.exp(math.log(3.0) * positions)
    row_scale = jnp.exp(jax.random.uniform(keys[1], (ROWS,), jnp.float32, math.log(0.4), math.log(4.0)))
    col_scale = jnp.exp(jax.random.uniform(keys[2], (TIME,), jnp.float32, math.log(0.4), math.log(4.0)))
    values = noise * (ramp * row_scale)[:, None] * col_scale[None, :]
    values = jnp.clip(values, -90.0, 90.0)
    return values.astype(jnp.bfloat16)


def levels(stream_key, dims, cuts, low, top_value):
    def one(position, parts):
        heights = jax.random.uniform(jax.random.fold_in(jax.random.fold_in(stream_key, 6), position), (parts,), jnp.float32, low / len(cuts), top_value / len(cuts))
        return jnp.repeat(jnp.exp(heights), dims[position] // parts).reshape((-1,) + (1,) * (len(dims) - position - 1))

    gain = one(*cuts[0])
    for cut in cuts[1:]:
        gain = gain * one(*cut)
    return gain


def scatter_about(key, dims, scale, limit, pieces=(), held_as=jnp.bfloat16):
    drawn = scale * jax.random.normal(key, dims, jnp.float32)
    if pieces:
        drawn = drawn * levels(key, dims, pieces, -0.22, 0.18)
    return jnp.clip(drawn, -limit, limit).astype(held_as)


def setup_inputs(seed: int = 0, part: int = 0) -> dict:
    arg_keys = jax.random.split(jax.random.key(seed), 3)
    part_splits = jax.random.split(jax.random.fold_in(arg_keys[2], part), 3)
    series_data = draw_series_data(jax.random.fold_in(jax.random.fold_in(arg_keys[2], part), 71), part)
    sketch_matrix = scatter_about(part_splits[1], (TIME, RANK), TIME ** -0.5, 0.1875, ((0, 16),))
    return dict(series_data=series_data, sketch_matrix=sketch_matrix)


def orthonormal(panel_rows):
    gram_sum = jnp.dot(panel_rows.T.astype(jnp.float32), panel_rows.astype(jnp.float32), precision=lax.Precision.HIGHEST, preferred_element_type=jnp.float32) / ROWS
    lower_factor = jnp.linalg.cholesky(gram_sum)
    inverse = jax.scipy.linalg.solve_triangular(lower_factor, jnp.eye(RANK, dtype=jnp.float32), lower=True)
    return jnp.dot(panel_rows.astype(jnp.float32), inverse.T.astype(jnp.float32), precision=lax.Precision.HIGHEST, preferred_element_type=jnp.float32).astype(jnp.bfloat16)

def project_back(series_data, basis):
    factor = math.sqrt(TIME) / ROWS
    summed = lax.dot_general(series_data.astype(jnp.float32), basis.astype(jnp.float32), (((0,), (0,)), ((), ())), preferred_element_type=jnp.float32)
    return (summed * factor).astype(jnp.bfloat16)

def reference(series_data, sketch_matrix):
    sketch = jnp.dot(series_data.astype(jnp.float32), sketch_matrix.astype(jnp.float32), preferred_element_type=jnp.float32)
    basis = orthonormal(sketch)
    back = project_back(series_data, basis)
    power = jnp.dot(series_data.astype(jnp.float32), back.astype(jnp.float32), preferred_element_type=jnp.float32)
    range_basis = orthonormal(power)
    coefficients = project_back(series_data, range_basis)
    return (range_basis, coefficients)
```

```python
import math

import jax
import jax.numpy as jnp
from jax import lax
from jax.sharding import PartitionSpec as P

AXIS = "series"
EDGE = 256
CHAINS = 2


def exchange(value, distance):
    n = lax.axis_size(AXIS)
    return lax.ppermute(value, AXIS, [(i, i ^ distance) for i in range(n)])


def piece(value, index, count):
    rows = value.shape[0] // count
    return lax.dynamic_slice_in_dim(value, index * rows, rows, 0)


def scatter_stage(value, low, count):
    me = (lax.axis_index(AXIS) >> low) & (count - 1)
    got = [exchange(piece(value, me ^ k, count), k << low) for k in range(1, count)]
    total = piece(value, me, count)
    for item in got:
        total = total + item
    return total


def gather_stage(value, low, count):
    me = (lax.axis_index(AXIS) >> low) & (count - 1)
    got = [value] + [exchange(value, k << low) for k in range(1, count)]
    if count == 2:
        return jnp.where(me == 0, jnp.concatenate(got), jnp.concatenate(got[::-1]))
    rows = value.shape[0]
    out = jnp.zeros((count * rows,) + value.shape[1:], value.dtype)
    for k in range(count):
        out = lax.dynamic_update_slice_in_dim(out, got[k], (me ^ k) * rows, 0)
    return out


def stages():
    n = lax.axis_size(AXIS)
    return [(0, 2), (1, 2), (2, n // 4)]


def sum_everywhere(value):
    for low, count in stages():
        value = scatter_stage(value, low, count)
    for low, count in reversed(stages()):
        value = gather_stage(value, low, count)
    return value


def gather_rows(value):
    for low, count in stages():
        value = gather_stage(value, low, count)
    return value


def exact(a, b, contract):
    return lax.dot_general(
        a.astype(jnp.float32),
        b.astype(jnp.float32),
        ((contract[0], contract[1]), ((), ())),
        precision=lax.Precision.HIGHEST,
        preferred_element_type=jnp.float32,
    )


def inverse_factor(gram):
    lower_factor = jnp.linalg.cholesky(gram)
    identity_k = jnp.eye(gram.shape[0], dtype=jnp.float32)
    return jax.scipy.linalg.solve_triangular(lower_factor, identity_k, lower=True)


def body(series_data, sketch_matrix):
    devices_here = lax.axis_size(AXIS)
    rows_total = series_data.shape[0] * devices_here
    local_steps = sketch_matrix.shape[0]
    time_steps = local_steps * devices_here
    factor = math.sqrt(time_steps) / rows_total
    nb = time_steps // EDGE

    sketch_all = gather_rows(sketch_matrix)

    blocks = []
    for i in range(nb):
        row = lax.dot_general(
            series_data[:, i * EDGE : (i + 1) * EDGE],
            series_data[:, : (i + 1) * EDGE],
            (((0,), (0,)), ((), ())),
            preferred_element_type=jnp.float32,
        )
        blocks += [row[:, j * EDGE : (j + 1) * EDGE] for j in range(i + 1)]
    per = len(blocks) // CHAINS
    summed = [
        sum_everywhere(jnp.concatenate(blocks[c * per : (c + 1) * per])) for c in range(CHAINS)
    ]
    flat = [s[k * EDGE : (k + 1) * EDGE] for s in summed for k in range(per)]
    at = lambda i, j: flat[i * (i + 1) // 2 + j] if j <= i else flat[j * (j + 1) // 2 + i].T
    moment = jnp.concatenate(
        [jnp.concatenate([at(i, j) for j in range(nb)], axis=1) for i in range(nb)]
    )

    y = exact(moment, sketch_all, ((1,), (0,)))
    inverse = inverse_factor(exact(sketch_all, y, ((0,), (0,))) / rows_total)
    back = (exact(y, inverse, ((1,), (1,))) * factor).astype(jnp.bfloat16)
    z = exact(moment, back, ((1,), (0,)))
    inverse2 = inverse_factor(exact(back, z, ((0,), (0,))) / rows_total)
    power = jnp.dot(series_data, back, preferred_element_type=jnp.float32)
    range_basis = exact(power, inverse2, ((1,), (1,))).astype(jnp.bfloat16)
    mine = lax.dynamic_slice_in_dim(z, lax.axis_index(AXIS) * local_steps, local_steps, 0)
    coefficients = (exact(mine, inverse2, ((1,), (1,))) * factor).astype(jnp.bfloat16)
    return (range_basis, coefficients)


def solution(mesh):
    in_specs = (P(("groups", "series"), None), P(("groups", "series"), None))
    out_specs = (P(("groups", "series"), None), P(("groups", "series"), None))
    return jax.shard_map(body, mesh=mesh, in_specs=in_specs, out_specs=out_specs, check_vma=False)
```

```python
import functools
import math

import jax
import jax.numpy as jnp
from jax import lax
from jax.experimental import pallas as pl
from jax.experimental.pallas import tpu as pltpu
from jax.sharding import PartitionSpec as P

AXIS = "series"
EDGE = 256
HALF = 128
PIVOTS = 32
CHAINS = 2
F32 = jnp.float32
BF16 = jnp.bfloat16


def exchange(value, distance):
    n = lax.axis_size(AXIS)
    return lax.ppermute(value, AXIS, [(i, i ^ distance) for i in range(n)])


def piece(value, index, count):
    rows = value.shape[0] // count
    return lax.dynamic_slice_in_dim(value, index * rows, rows, 0)


def scatter_stage(value, low, count):
    me = (lax.axis_index(AXIS) >> low) & (count - 1)
    got = [exchange(piece(value, me ^ k, count), k << low) for k in range(1, count)]
    total = piece(value, me, count)
    for item in got:
        total = total + item
    return total


def gather_stage(value, low, count):
    me = (lax.axis_index(AXIS) >> low) & (count - 1)
    got = [value] + [exchange(value, k << low) for k in range(1, count)]
    if count == 2:
        return jnp.where(me == 0, jnp.concatenate(got), jnp.concatenate(got[::-1]))
    rows = value.shape[0]
    out = jnp.zeros((count * rows,) + value.shape[1:], value.dtype)
    for k in range(count):
        out = lax.dynamic_update_slice_in_dim(out, got[k], (me ^ k) * rows, 0)
    return out


def stages():
    n = lax.axis_size(AXIS)
    return [(0, 2), (1, 2), (2, n // 4)]


def sum_everywhere(value):
    for low, count in stages():
        value = scatter_stage(value, low, count)
    for low, count in reversed(stages()):
        value = gather_stage(value, low, count)
    return value


def gather_rows(value):
    for low, count in stages():
        value = gather_stage(value, low, count)
    return value


def layout(time_steps):
    nb = time_steps // EDGE
    off = [(i, j) for i in range(nb) for j in range(i)]
    chains = [[] for _ in range(CHAINS)]
    for k, ij in enumerate(off):
        chains[k * CHAINS // len(off)].append(ij)
    for i in range(nb):
        chains[i * CHAINS // nb].append((i, i))
    return chains


def chain_rows(chain):
    return sum(EDGE if i != j else EDGE * 3 // 4 for i, j in chain)


def three(value):
    high = value.astype(BF16)
    rest = value - high.astype(F32)
    mid = rest.astype(BF16)
    low = (rest - mid.astype(F32)).astype(BF16)
    return high, mid, low


def product(a, b, contract=((1,), (0,)), precision=None):
    return lax.dot_general(
        a, b, (contract, ((), ())), precision=precision, preferred_element_type=F32
    )


def moment_kernel(chains, a_ref, *out_refs):
    for chain, out in zip(chains, out_refs):
        row = 0
        for i, j in chain:
            left = a_ref[:, i * EDGE : (i + 1) * EDGE]
            block = product(left, a_ref[:, j * EDGE : (j + 1) * EDGE], ((0,), (0,)))
            if i != j:
                out[row : row + EDGE, :] = block
                row += EDGE
            else:
                out[row : row + HALF, :HALF] = block[:HALF, :HALF]
                out[row : row + HALF, HALF:] = block[HALF:, HALF:]
                out[row + HALF : row + HALF + HALF // 2, :HALF] = block[HALF : HALF + HALF // 2, :HALF]
                out[row + HALF : row + HALF + HALF // 2, HALF:] = block[HALF + HALF // 2 :, :HALF]
                row += EDGE * 3 // 4


def unpack(chains, refs, store):
    for chain, ref in zip(chains, refs):
        row = 0
        for i, j in chain:
            if i != j:
                block = ref[row : row + EDGE, :]
                row += EDGE
                store(i, j, block)
                store(j, i, block.T)
            else:
                first = ref[row : row + HALF, :HALF]
                last = ref[row : row + HALF, HALF:]
                tail = ref[row + HALF : row + HALF + HALF // 2, :]
                cross = jnp.concatenate([tail[:, :HALF], tail[:, HALF:]], axis=0)
                row += EDGE * 3 // 4
                store(
                    i,
                    i,
                    jnp.concatenate(
                        [
                            jnp.concatenate([first, cross.T], axis=1),
                            jnp.concatenate([cross, last], axis=1),
                        ],
                        axis=0,
                    ),
                )


def inverse_factor(x_ref, w_ref, beside=None):
    n = x_ref.shape[0]
    groups = PIVOTS // 8
    tiles = n // 128
    lane = lax.broadcasted_iota(jnp.int32, (8, 128), 1)
    sub = lax.broadcasted_iota(jnp.int32, (8, 128), 0)
    for k in range(n // PIVOTS):
        o = PIVOTS * k
        home, lo = o // 128, o % 128
        panel = [
            [x_ref[o + 8 * g : o + 8 * g + 8, 128 * t : 128 * t + 128] for t in range(tiles)]
            for g in range(groups)
        ]
        col = {
            (i, g): jnp.broadcast_to(panel[g][home][:, lo + i : lo + i + 1], (8, 128))
            for i in range(PIVOTS)
            for g in range(i // 8, groups)
        }
        in_block = (lane >= lo) & (lane < lo + PIVOTS)
        for g in range(groups):
            unit = jnp.where(lane - lo == sub + 8 * g, 1.0, 0.0)
            panel[g][home] = jnp.where(in_block, unit, panel[g][home])
        if beside is not None:
            beside(k)
        for j in range(PIVOTS):
            gj, s = j // 8, j % 8
            scale = lax.rsqrt(jnp.broadcast_to(col[j, gj][s : s + 1, :], (8, 128)))
            low = {g: col[j, g] * scale for g in range(gj, groups)}
            for i in range(j + 1, PIVOTS):
                other = jnp.broadcast_to(low[i // 8][i % 8 : i % 8 + 1, :], (8, 128))
                for g in range(i // 8, groups):
                    col[i, g] = col[i, g] - low[g] * other
            low[gj] = jnp.where(sub > s, low[gj], 0.0)
            for t in range(tiles):
                row = jnp.broadcast_to(panel[gj][t][s : s + 1, :], (8, 128)) * scale
                for g in range(gj, groups):
                    left = panel[g][t] - low[g] * row
                    panel[g][t] = jnp.where(sub == s, row, left) if g == gj else left
        for g in range(groups):
            for t in range(tiles):
                part = panel[g][t]
                if t > home:
                    part = jnp.zeros_like(part)
                elif t == home:
                    part = jnp.where(lane < lo + PIVOTS, part, 0.0)
                w_ref[o + 8 * g : o + 8 * g + 8, 128 * t : 128 * t + 128] = part
        nxt = o + PIVOTS
        if nxt < n:
            rows = jnp.concatenate([jnp.concatenate(p, axis=1) for p in panel], axis=0)
            first = nxt // 128 * 128
            a, b, c = three(rows)
            left = jnp.concatenate([a, a, a, b, b, c], axis=0)[:, first:]
            right = jnp.concatenate([a, b, c, a, b, a], axis=0)
            update = product(left, right, ((0,), (0,)))
            old = x_ref[nxt:, :]
            column = lax.broadcasted_iota(jnp.int32, old.shape, 1)
            old = jnp.where((column >= o) & (column < nxt), 0.0, old)
            x_ref[nxt:, :] = old - update[nxt - first :, :]


def finish_kernel(
    chains, rows_total, factor, me_ref, sketch_ref, a_hbm, *refs
):
    chain_refs, refs = refs[: len(chains)], refs[len(chains) :]
    range_ref, coef_ref, moment, a_ref, power, y_ref, back_ref, x_ref, w_ref, sem = refs
    time_steps, rank = sketch_ref.shape
    nb = time_steps // EDGE
    fetch = pltpu.make_async_copy(a_hbm, a_ref, sem)
    fetch.start()

    def store(i, j, block):
        for p, part in enumerate(three(block)):
            moment[p, i * EDGE : (i + 1) * EDGE, j * EDGE : (j + 1) * EDGE] = part

    unpack(chains, chain_refs, store)

    def apply_moment(right_ref):
        for i in range(nb):
            band = slice(i * EDGE, (i + 1) * EDGE)
            total = product(moment[0, band, :], right_ref[...])
            total = total + product(moment[1, band, :], right_ref[...])
            y_ref[band, :] = total + product(moment[2, band, :], right_ref[...])

    def gram(left_ref):
        wide = product(left_ref[...], jnp.concatenate(three(y_ref[...]), axis=1), ((0,), (0,)))
        x_ref[...] = (wide[:, :rank] + wide[:, rank : 2 * rank] + wide[:, 2 * rank :]) / rows_total

    high = lax.Precision.HIGHEST
    apply_moment(sketch_ref)
    gram(sketch_ref)
    inverse_factor(x_ref, w_ref)
    for i in range(nb):
        band = slice(i * EDGE, (i + 1) * EDGE)
        back_ref[band, :] = (
            product(y_ref[band, :], w_ref[...], ((1,), (1,)), high) * factor
        ).astype(BF16)
    apply_moment(back_ref)
    gram(back_ref)
    fetch.wait()
    panels = rank // PIVOTS
    share = a_ref.shape[0] // panels

    def some_power(k):
        band = slice(k * share, (k + 1) * share)
        power[band, :] = product(a_ref[band, :], back_ref[...])

    inverse_factor(x_ref, w_ref, some_power)
    for k in range(panels):
        band = slice(k * share, (k + 1) * share)
        range_ref[band, :] = product(power[band, :], w_ref[...], ((1,), (1,)), high).astype(BF16)
    steps = coef_ref.shape[0]
    mine = y_ref[pl.ds(pl.multiple_of(me_ref[0] * steps, steps), steps), :]
    coef_ref[...] = (product(mine, w_ref[...], ((1,), (1,)), high) * factor).astype(BF16)


def body(series_data, sketch_matrix):
    devices_here = lax.axis_size(AXIS)
    local_rows = series_data.shape[0]
    rows_total = local_rows * devices_here
    local_steps, rank = sketch_matrix.shape
    time_steps = local_steps * devices_here
    factor = math.sqrt(time_steps) / rows_total
    chains = layout(time_steps)
    vmem = pl.BlockSpec(memory_space=pltpu.VMEM)

    sketch_all = gather_rows(sketch_matrix)
    partial = pl.pallas_call(
        functools.partial(moment_kernel, chains),
        out_shape=[jax.ShapeDtypeStruct((chain_rows(c), EDGE), F32) for c in chains],
        in_specs=[vmem],
        out_specs=[vmem] * len(chains),
        compiler_params=pltpu.CompilerParams(vmem_limit_bytes=20 << 20),
    )(series_data)
    summed = [sum_everywhere(p) for p in partial]
    me = lax.axis_index(AXIS).astype(jnp.int32).reshape(1)
    return tuple(
        pl.pallas_call(
            functools.partial(finish_kernel, chains, rows_total, factor),
            out_shape=[
                jax.ShapeDtypeStruct((local_rows, rank), BF16),
                jax.ShapeDtypeStruct((local_steps, rank), BF16),
            ],
            in_specs=[
                pl.BlockSpec(memory_space=pltpu.SMEM),
                vmem,
                pl.BlockSpec(memory_space=pl.ANY),
            ]
            + [vmem] * len(chains),
            out_specs=[vmem, vmem],
            scratch_shapes=[
                pltpu.VMEM((3, time_steps, time_steps), BF16),
                pltpu.VMEM(series_data.shape, BF16),
                pltpu.VMEM((local_rows, rank), F32),
                pltpu.VMEM((time_steps, rank), F32),
                pltpu.VMEM((time_steps, rank), BF16),
                pltpu.VMEM((rank, rank), F32),
                pltpu.VMEM((rank, rank), F32),
                pltpu.SemaphoreType.DMA,
            ],
            compiler_params=pltpu.CompilerParams(vmem_limit_bytes=40 << 20),
        )(me, sketch_all, series_data, *summed)
    )


def solution(mesh):
    in_specs = (P(("groups", "series"), None), P(("groups", "series"), None))
    out_specs = (P(("groups", "series"), None), P(("groups", "series"), None))
    return jax.shard_map(body, mesh=mesh, in_specs=in_specs, out_specs=out_specs, check_vma=False)
```

```python
import functools
import math

import jax
import jax.numpy as jnp
from jax import lax
from jax.experimental import pallas as pl
from jax.experimental.pallas import tpu as pltpu
from jax.sharding import PartitionSpec as P

AXIS = "series"
EDGE = 256
HALF = 128
PIVOTS = 32
CHAINS = 2
F32 = jnp.float32
BF16 = jnp.bfloat16


def exchange(value, distance):
    n = lax.axis_size(AXIS)
    return lax.ppermute(value, AXIS, [(i, i ^ distance) for i in range(n)])


def piece(value, index, count):
    rows = value.shape[0] // count
    return lax.dynamic_slice_in_dim(value, index * rows, rows, 0)


def scatter_stage(value, low, count):
    me = (lax.axis_index(AXIS) >> low) & (count - 1)
    got = [exchange(piece(value, me ^ k, count), k << low) for k in range(1, count)]
    total = piece(value, me, count)
    for item in got:
        total = total + item
    return total


def gather_stage(value, low, count):
    me = (lax.axis_index(AXIS) >> low) & (count - 1)
    got = [value] + [exchange(value, k << low) for k in range(1, count)]
    if count == 2:
        return jnp.where(me == 0, jnp.concatenate(got), jnp.concatenate(got[::-1]))
    rows = value.shape[0]
    out = jnp.zeros((count * rows,) + value.shape[1:], value.dtype)
    for k in range(count):
        out = lax.dynamic_update_slice_in_dim(out, got[k], (me ^ k) * rows, 0)
    return out


def stages():
    n = lax.axis_size(AXIS)
    return [(0, 2), (1, 2), (2, n // 4)]


def tie(value, other):
    return lax.optimization_barrier((value, other))


def sum_everywhere(parts, rows):
    (c, _), (y, _), (z, others) = stages()
    own = rows.shape[0]
    parts = [scatter_stage(p, c, 2) for p in parts]
    rows = gather_stage(rows, z, others)
    parts = [scatter_stage(p, y, 2) for p in parts]
    parts[0], rows = tie(parts[0], rows)
    rows = gather_stage(rows, y, 2)
    parts = [scatter_stage(p, z, others) for p in parts]
    parts[0], rows = tie(parts[0], rows)
    rows = gather_stage(rows, c, 2)
    parts = [gather_stage(p, z, others) for p in parts]
    parts[0], rows = tie(parts[0], rows)
    parts = [gather_stage(p, y, 2) for p in parts]
    parts = [gather_stage(p, c, 2) for p in parts]
    rows = rows.reshape(2, 2, others, own, -1).transpose(2, 1, 0, 3, 4)
    return parts, rows.reshape(4 * others * own, -1)


def layout(time_steps):
    nb = time_steps // EDGE
    off = [(i, j) for i in range(nb) for j in range(i)]
    chains = [[] for _ in range(CHAINS)]
    for k, ij in enumerate(off):
        chains[k * CHAINS // len(off)].append(ij)
    for i in range(nb):
        chains[i * CHAINS // nb].append((i, i))
    return chains


def chain_rows(chain):
    return sum(EDGE if i != j else EDGE * 3 // 4 for i, j in chain)


def three(value):
    high = value.astype(BF16)
    rest = value - high.astype(F32)
    mid = rest.astype(BF16)
    low = (rest - mid.astype(F32)).astype(BF16)
    return high, mid, low


def product(a, b, contract=((1,), (0,)), precision=None):
    return lax.dot_general(
        a, b, (contract, ((), ())), precision=precision, preferred_element_type=F32
    )


def moment_kernel(chains, a_hbm, *refs):
    out_refs, (a_ref, sems) = refs[: len(chains)], refs[len(chains) :]
    nb = a_ref.shape[0]
    fetches = [
        pltpu.make_async_copy(a_hbm.at[:, pl.ds(i * EDGE, EDGE)], a_ref.at[i], sems.at[i])
        for i in range(nb)
    ]
    for fetch in fetches:
        fetch.start()
    where = {}
    for chain, out in zip(chains, out_refs):
        row = 0
        for i, j in chain:
            where[i, j] = out, row
            row += EDGE if i != j else EDGE * 3 // 4
    for i in range(nb):
        fetches[i].wait()
        left = a_ref[i]
        for j in range(i + 1):
            block = product(left, a_ref[j], ((0,), (0,)))
            out, row = where[i, j]
            if i != j:
                out[row : row + EDGE, :] = block
            else:
                cut = HALF + HALF // 2
                out[row : row + HALF, :HALF] = block[:HALF, :HALF]
                out[row : row + HALF, HALF:] = block[HALF:, HALF:]
                out[row + HALF : row + cut, :HALF] = block[HALF:cut, :HALF]
                out[row + HALF : row + cut, HALF:] = block[cut:, :HALF]


def unpack(chains, refs, store):
    for chain, ref in zip(chains, refs):
        row = 0
        for i, j in chain:
            if i != j:
                block = ref[row : row + EDGE, :]
                row += EDGE
                store(i, j, block)
                store(j, i, block.T)
            else:
                first = ref[row : row + HALF, :HALF]
                last = ref[row : row + HALF, HALF:]
                tail = ref[row + HALF : row + HALF + HALF // 2, :]
                cross = jnp.concatenate([tail[:, :HALF], tail[:, HALF:]], axis=0)
                row += EDGE * 3 // 4
                store(
                    i,
                    i,
                    jnp.concatenate(
                        [
                            jnp.concatenate([first, cross.T], axis=1),
                            jnp.concatenate([cross, last], axis=1),
                        ],
                        axis=0,
                    ),
                )


def inverse_factor(x_ref, w_ref, beside=None):
    n = x_ref.shape[0]
    groups = PIVOTS // 8
    tiles = n // 128
    lane = lax.broadcasted_iota(jnp.int32, (8, 128), 1)
    sub = lax.broadcasted_iota(jnp.int32, (8, 128), 0)
    for k in range(n // PIVOTS):
        o = PIVOTS * k
        home, lo = o // 128, o % 128
        panel = [
            [x_ref[o + 8 * g : o + 8 * g + 8, 128 * t : 128 * t + 128] for t in range(tiles)]
            for g in range(groups)
        ]
        col = {
            (i, g): jnp.broadcast_to(panel[g][home][:, lo + i : lo + i + 1], (8, 128))
            for i in range(PIVOTS)
            for g in range(i // 8, groups)
        }
        in_block = (lane >= lo) & (lane < lo + PIVOTS)
        for g in range(groups):
            unit = jnp.where(lane - lo == sub + 8 * g, 1.0, 0.0)
            panel[g][home] = jnp.where(in_block, unit, panel[g][home])
        if beside is not None:
            beside(k)
        for j in range(PIVOTS):
            gj, s = j // 8, j % 8
            scale = lax.rsqrt(jnp.broadcast_to(col[j, gj][s : s + 1, :], (8, 128)))
            low = {g: col[j, g] * scale for g in range(gj, groups)}
            for i in range(j + 1, PIVOTS):
                other = jnp.broadcast_to(low[i // 8][i % 8 : i % 8 + 1, :], (8, 128))
                for g in range(i // 8, groups):
                    col[i, g] = col[i, g] - low[g] * other
            low[gj] = jnp.where(sub > s, low[gj], 0.0)
            for t in range(tiles):
                row = jnp.broadcast_to(panel[gj][t][s : s + 1, :], (8, 128)) * scale
                for g in range(gj, groups):
                    left = panel[g][t] - low[g] * row
                    panel[g][t] = jnp.where(sub == s, row, left) if g == gj else left
        for g in range(groups):
            for t in range(tiles):
                part = panel[g][t]
                if t > home:
                    part = jnp.zeros_like(part)
                elif t == home:
                    part = jnp.where(lane < lo + PIVOTS, part, 0.0)
                w_ref[o + 8 * g : o + 8 * g + 8, 128 * t : 128 * t + 128] = part
        nxt = o + PIVOTS
        if nxt < n:
            rows = jnp.concatenate([jnp.concatenate(p, axis=1) for p in panel], axis=0)
            first = nxt // 128 * 128
            a, b, c = three(rows)
            left = jnp.concatenate([a, a, a, b, b, c], axis=0)[:, first:]
            right = jnp.concatenate([a, b, c, a, b, a], axis=0)
            update = product(left, right, ((0,), (0,)))
            old = x_ref[nxt:, :]
            column = lax.broadcasted_iota(jnp.int32, old.shape, 1)
            old = jnp.where((column >= o) & (column < nxt), 0.0, old)
            x_ref[nxt:, :] = old - update[nxt - first :, :]


def finish_kernel(
    chains, rows_total, factor, me_ref, sketch_ref, a_hbm, *refs
):
    chain_refs, refs = refs[: len(chains)], refs[len(chains) :]
    range_ref, coef_ref, moment, a_ref, power, y_ref, back_ref, x_ref, w_ref, sem = refs
    time_steps, rank = sketch_ref.shape
    nb = time_steps // EDGE
    fetch = pltpu.make_async_copy(a_hbm, a_ref, sem)
    fetch.start()

    def store(i, j, block):
        for p, part in enumerate(three(block)):
            moment[p, i * EDGE : (i + 1) * EDGE, j * EDGE : (j + 1) * EDGE] = part

    unpack(chains, chain_refs, store)

    def apply_moment(right_ref):
        for i in range(nb):
            band = slice(i * EDGE, (i + 1) * EDGE)
            total = product(moment[0, band, :], right_ref[...])
            total = total + product(moment[1, band, :], right_ref[...])
            y_ref[band, :] = total + product(moment[2, band, :], right_ref[...])

    def gram(left_ref):
        wide = product(left_ref[...], jnp.concatenate(three(y_ref[...]), axis=1), ((0,), (0,)))
        x_ref[...] = (wide[:, :rank] + wide[:, rank : 2 * rank] + wide[:, 2 * rank :]) / rows_total

    high = lax.Precision.HIGHEST
    apply_moment(sketch_ref)
    gram(sketch_ref)
    inverse_factor(x_ref, w_ref)
    for i in range(nb):
        band = slice(i * EDGE, (i + 1) * EDGE)
        back_ref[band, :] = (
            product(y_ref[band, :], w_ref[...], ((1,), (1,)), high) * factor
        ).astype(BF16)
    apply_moment(back_ref)
    gram(back_ref)
    fetch.wait()
    panels = rank // PIVOTS
    share = a_ref.shape[0] // panels

    def some_power(k):
        band = slice(k * share, (k + 1) * share)
        power[band, :] = product(a_ref[band, :], back_ref[...])

    inverse_factor(x_ref, w_ref, some_power)
    for k in range(panels):
        band = slice(k * share, (k + 1) * share)
        range_ref[band, :] = product(power[band, :], w_ref[...], ((1,), (1,)), high).astype(BF16)
    steps = coef_ref.shape[0]
    mine = y_ref[pl.ds(pl.multiple_of(me_ref[0] * steps, steps), steps), :]
    coef_ref[...] = (product(mine, w_ref[...], ((1,), (1,)), high) * factor).astype(BF16)


def body(series_data, sketch_matrix):
    devices_here = lax.axis_size(AXIS)
    local_rows = series_data.shape[0]
    rows_total = local_rows * devices_here
    local_steps, rank = sketch_matrix.shape
    time_steps = local_steps * devices_here
    factor = math.sqrt(time_steps) / rows_total
    chains = layout(time_steps)
    vmem = pl.BlockSpec(memory_space=pltpu.VMEM)

    partial = pl.pallas_call(
        functools.partial(moment_kernel, chains),
        out_shape=[jax.ShapeDtypeStruct((chain_rows(c), EDGE), F32) for c in chains],
        in_specs=[pl.BlockSpec(memory_space=pltpu.HBM)],
        out_specs=[vmem] * len(chains),
        scratch_shapes=[
            pltpu.VMEM((time_steps // EDGE, local_rows, EDGE), BF16),
            pltpu.SemaphoreType.DMA((time_steps // EDGE,)),
        ],
        compiler_params=pltpu.CompilerParams(vmem_limit_bytes=20 << 20),
    )(series_data)
    summed, sketch_all = sum_everywhere(list(partial), sketch_matrix)
    me = lax.axis_index(AXIS).astype(jnp.int32).reshape(1)
    return tuple(
        pl.pallas_call(
            functools.partial(finish_kernel, chains, rows_total, factor),
            out_shape=[
                jax.ShapeDtypeStruct((local_rows, rank), BF16),
                jax.ShapeDtypeStruct((local_steps, rank), BF16),
            ],
            in_specs=[
                pl.BlockSpec(memory_space=pltpu.SMEM),
                vmem,
                pl.BlockSpec(memory_space=pltpu.HBM),
            ]
            + [vmem] * len(chains),
            out_specs=[vmem, vmem],
            scratch_shapes=[
                pltpu.VMEM((3, time_steps, time_steps), BF16),
                pltpu.VMEM(series_data.shape, BF16),
                pltpu.VMEM((local_rows, rank), F32),
                pltpu.VMEM((time_steps, rank), F32),
                pltpu.VMEM((time_steps, rank), BF16),
                pltpu.VMEM((rank, rank), F32),
                pltpu.VMEM((rank, rank), F32),
                pltpu.SemaphoreType.DMA,
            ],
            compiler_params=pltpu.CompilerParams(vmem_limit_bytes=40 << 20),
        )(me, sketch_all, series_data, *summed)
    )


def solution(mesh):
    in_specs = (P(("groups", "series"), None), P(("groups", "series"), None))
    out_specs = (P(("groups", "series"), None), P(("groups", "series"), None))
    return jax.shard_map(body, mesh=mesh, in_specs=in_specs, out_specs=out_specs, check_vma=False)
```

```python
import functools
import math

import jax
import jax.numpy as jnp
from jax import lax
from jax.experimental import pallas as pl
from jax.experimental.pallas import tpu as pltpu
from jax.sharding import PartitionSpec as P

AXIS = "series"
EDGE = 256
HALF = 128
PIVOTS = 32
CHAINS = 2
F32 = jnp.float32
BF16 = jnp.bfloat16


def exchange(value, distance):
    n = lax.axis_size(AXIS)
    return lax.ppermute(value, AXIS, [(i, i ^ distance) for i in range(n)])


def piece(value, index, count):
    rows = value.shape[0] // count
    return lax.dynamic_slice_in_dim(value, index * rows, rows, 0)


def scatter_stage(value, low, count):
    me = (lax.axis_index(AXIS) >> low) & (count - 1)
    got = [exchange(piece(value, me ^ k, count), k << low) for k in range(1, count)]
    total = piece(value, me, count)
    for item in got:
        total = total + item
    return total


def gather_stage(value, low, count):
    me = (lax.axis_index(AXIS) >> low) & (count - 1)
    got = [value] + [exchange(value, k << low) for k in range(1, count)]
    if count == 2:
        return jnp.where(me == 0, jnp.concatenate(got), jnp.concatenate(got[::-1]))
    rows = value.shape[0]
    out = jnp.zeros((count * rows,) + value.shape[1:], value.dtype)
    for k in range(count):
        out = lax.dynamic_update_slice_in_dim(out, got[k], (me ^ k) * rows, 0)
    return out


def stages():
    n = lax.axis_size(AXIS)
    return [(0, 2), (1, 4), (3, n // 8)]


def tie(value, other):
    return lax.optimization_barrier((value, other))


def widen(rows, low, count):
    return jnp.concatenate([rows] + [exchange(rows, k << low) for k in range(1, count)])


def sum_everywhere(parts, rows):
    core, square, far = stages()
    parts = [scatter_stage(p, *core) for p in parts]
    rows = widen(rows, *far)
    parts = [scatter_stage(p, *square) for p in parts]
    parts[0], rows = tie(parts[0], rows)
    parts = [scatter_stage(p, *far) for p in parts]
    rows = widen(rows, *square)
    parts = [gather_stage(p, *far) for p in parts]
    parts[0], rows = tie(parts[0], rows)
    rows = widen(rows, *core)
    parts = [gather_stage(p, *square) for p in parts]
    parts = [gather_stage(p, *core) for p in parts]
    return parts, rows


def layout(time_steps):
    nb = time_steps // EDGE
    off = [(i, j) for i in range(nb) for j in range(i)]
    chains = [[] for _ in range(CHAINS)]
    for k, ij in enumerate(off):
        chains[k * CHAINS // len(off)].append(ij)
    for i in range(nb):
        chains[i * CHAINS // nb].append((i, i))
    return chains


def chain_rows(chain):
    return sum(EDGE if i != j else EDGE * 3 // 4 for i, j in chain)


def three(value):
    high = value.astype(BF16)
    rest = value - high.astype(F32)
    mid = rest.astype(BF16)
    low = (rest - mid.astype(F32)).astype(BF16)
    return high, mid, low


def product(a, b, contract=((1,), (0,)), precision=None):
    return lax.dot_general(
        a, b, (contract, ((), ())), precision=precision, preferred_element_type=F32
    )


def moment_kernel(chains, a_ref, *out_refs):
    for chain, out in zip(chains, out_refs):
        row = 0
        for i, j in chain:
            left = a_ref[:, i * EDGE : (i + 1) * EDGE]
            block = product(left, a_ref[:, j * EDGE : (j + 1) * EDGE], ((0,), (0,)))
            if i != j:
                out[row : row + EDGE, :] = block
                row += EDGE
            else:
                cut = HALF + HALF // 2
                out[row : row + HALF, :HALF] = block[:HALF, :HALF]
                out[row : row + HALF, HALF:] = block[HALF:, HALF:]
                out[row + HALF : row + cut, :HALF] = block[HALF:cut, :HALF]
                out[row + HALF : row + cut, HALF:] = block[cut:, :HALF]
                row += EDGE * 3 // 4


def unpack(chains, refs, store):
    for chain, ref in zip(chains, refs):
        row = 0
        for i, j in chain:
            if i != j:
                block = ref[row : row + EDGE, :]
                row += EDGE
                store(i, j, block)
                store(j, i, block.T)
            else:
                first = ref[row : row + HALF, :HALF]
                last = ref[row : row + HALF, HALF:]
                tail = ref[row + HALF : row + HALF + HALF // 2, :]
                cross = jnp.concatenate([tail[:, :HALF], tail[:, HALF:]], axis=0)
                row += EDGE * 3 // 4
                store(
                    i,
                    i,
                    jnp.concatenate(
                        [
                            jnp.concatenate([first, cross.T], axis=1),
                            jnp.concatenate([cross, last], axis=1),
                        ],
                        axis=0,
                    ),
                )


def inverse_factor(x_ref, w_ref, beside=None):
    n = x_ref.shape[0]
    groups = PIVOTS // 8
    tiles = n // 128
    lane = lax.broadcasted_iota(jnp.int32, (8, 128), 1)
    sub = lax.broadcasted_iota(jnp.int32, (8, 128), 0)
    for k in range(n // PIVOTS):
        o = PIVOTS * k
        home, lo = o // 128, o % 128
        panel = [
            [x_ref[o + 8 * g : o + 8 * g + 8, 128 * t : 128 * t + 128] for t in range(tiles)]
            for g in range(groups)
        ]
        col = {
            (i, g): jnp.broadcast_to(panel[g][home][:, lo + i : lo + i + 1], (8, 128))
            for i in range(PIVOTS)
            for g in range(i // 8, groups)
        }
        in_block = (lane >= lo) & (lane < lo + PIVOTS)
        for g in range(groups):
            unit = jnp.where(lane - lo == sub + 8 * g, 1.0, 0.0)
            panel[g][home] = jnp.where(in_block, unit, panel[g][home])
        if beside is not None:
            beside(k)
        for j in range(PIVOTS):
            gj, s = j // 8, j % 8
            scale = lax.rsqrt(jnp.broadcast_to(col[j, gj][s : s + 1, :], (8, 128)))
            low = {g: col[j, g] * scale for g in range(gj, groups)}
            for i in range(j + 1, PIVOTS):
                other = jnp.broadcast_to(low[i // 8][i % 8 : i % 8 + 1, :], (8, 128))
                for g in range(i // 8, groups):
                    col[i, g] = col[i, g] - low[g] * other
            low[gj] = jnp.where(sub > s, low[gj], 0.0)
            for t in range(tiles):
                row = jnp.broadcast_to(panel[gj][t][s : s + 1, :], (8, 128)) * scale
                for g in range(gj, groups):
                    left = panel[g][t] - low[g] * row
                    panel[g][t] = jnp.where(sub == s, row, left) if g == gj else left
        for g in range(groups):
            for t in range(tiles):
                part = panel[g][t]
                if t > home:
                    part = jnp.zeros_like(part)
                elif t == home:
                    part = jnp.where(lane < lo + PIVOTS, part, 0.0)
                w_ref[o + 8 * g : o + 8 * g + 8, 128 * t : 128 * t + 128] = part
        nxt = o + PIVOTS
        if nxt < n:
            rows = jnp.concatenate([jnp.concatenate(p, axis=1) for p in panel], axis=0)
            first = nxt // 128 * 128
            a, b, c = three(rows)
            left = jnp.concatenate([a, a, a, b, b, c], axis=0)[:, first:]
            right = jnp.concatenate([a, b, c, a, b, a], axis=0)
            update = product(left, right, ((0,), (0,)))
            old = x_ref[nxt:, :]
            column = lax.broadcasted_iota(jnp.int32, old.shape, 1)
            old = jnp.where((column >= o) & (column < nxt), 0.0, old)
            x_ref[nxt:, :] = old - update[nxt - first :, :]


def finish_kernel(
    chains, rows_total, factor, me_ref, sketch_ref, a_hbm, *refs
):
    chain_refs, refs = refs[: len(chains)], refs[len(chains) :]
    range_ref, coef_ref, moment, a_ref, power, y_ref, back_ref, x_ref, w_ref, sem = refs
    time_steps, rank = sketch_ref.shape
    steps = coef_ref.shape[0]
    nb = time_steps // EDGE
    fetch = pltpu.make_async_copy(a_hbm, a_ref, sem)
    fetch.start()

    devices = time_steps // steps
    for k in range(devices):
        others = devices // 8
        away = k % others * 8 + k // others % 4 * 2 + k // others // 4
        block = sketch_ref[k * steps : (k + 1) * steps, :].astype(F32)
        spot = lax.bitwise_xor(me_ref[0], jnp.int32(away)) * steps
        y_ref[pl.ds(pl.multiple_of(spot, steps), steps), :] = block
    sketch_ref = back_ref
    sketch_ref[...] = y_ref[...].astype(BF16)

    def store(i, j, block):
        for p, part in enumerate(three(block)):
            moment[p, i * EDGE : (i + 1) * EDGE, j * EDGE : (j + 1) * EDGE] = part

    unpack(chains, chain_refs, store)

    def apply_moment(right_ref):
        for i in range(nb):
            band = slice(i * EDGE, (i + 1) * EDGE)
            total = product(moment[0, band, :], right_ref[...])
            total = total + product(moment[1, band, :], right_ref[...])
            y_ref[band, :] = total + product(moment[2, band, :], right_ref[...])

    def gram(left_ref):
        wide = product(left_ref[...], jnp.concatenate(three(y_ref[...]), axis=1), ((0,), (0,)))
        x_ref[...] = (wide[:, :rank] + wide[:, rank : 2 * rank] + wide[:, 2 * rank :]) / rows_total

    high = lax.Precision.HIGHEST
    apply_moment(sketch_ref)
    gram(sketch_ref)
    inverse_factor(x_ref, w_ref)
    for i in range(nb):
        band = slice(i * EDGE, (i + 1) * EDGE)
        back_ref[band, :] = (
            product(y_ref[band, :], w_ref[...], ((1,), (1,)), high) * factor
        ).astype(BF16)
    apply_moment(back_ref)
    gram(back_ref)
    fetch.wait()
    panels = rank // PIVOTS
    share = a_ref.shape[0] // panels

    def some_power(k):
        band = slice(k * share, (k + 1) * share)
        power[band, :] = product(a_ref[band, :], back_ref[...])

    inverse_factor(x_ref, w_ref, some_power)
    for k in range(panels):
        band = slice(k * share, (k + 1) * share)
        range_ref[band, :] = product(power[band, :], w_ref[...], ((1,), (1,)), high).astype(BF16)
    mine = y_ref[pl.ds(pl.multiple_of(me_ref[0] * steps, steps), steps), :]
    coef_ref[...] = (product(mine, w_ref[...], ((1,), (1,)), high) * factor).astype(BF16)


def body(series_data, sketch_matrix):
    devices_here = lax.axis_size(AXIS)
    local_rows = series_data.shape[0]
    rows_total = local_rows * devices_here
    local_steps, rank = sketch_matrix.shape
    time_steps = local_steps * devices_here
    factor = math.sqrt(time_steps) / rows_total
    chains = layout(time_steps)
    vmem = pl.BlockSpec(memory_space=pltpu.VMEM)

    partial = pl.pallas_call(
        functools.partial(moment_kernel, chains),
        out_shape=[jax.ShapeDtypeStruct((chain_rows(c), EDGE), F32) for c in chains],
        in_specs=[vmem],
        out_specs=[vmem] * len(chains),
        compiler_params=pltpu.CompilerParams(vmem_limit_bytes=20 << 20),
    )(series_data)
    summed, sketch_all = sum_everywhere(list(partial), sketch_matrix)
    me = lax.axis_index(AXIS).astype(jnp.int32).reshape(1)
    return tuple(
        pl.pallas_call(
            functools.partial(finish_kernel, chains, rows_total, factor),
            out_shape=[
                jax.ShapeDtypeStruct((local_rows, rank), BF16),
                jax.ShapeDtypeStruct((local_steps, rank), BF16),
            ],
            in_specs=[
                pl.BlockSpec(memory_space=pltpu.SMEM),
                vmem,
                pl.BlockSpec(memory_space=pltpu.HBM),
            ]
            + [vmem] * len(chains),
            out_specs=[vmem, vmem],
            scratch_shapes=[
                pltpu.VMEM((3, time_steps, time_steps), BF16),
                pltpu.VMEM(series_data.shape, BF16),
                pltpu.VMEM((local_rows, rank), F32),
                pltpu.VMEM((time_steps, rank), F32),
                pltpu.VMEM((time_steps, rank), BF16),
                pltpu.VMEM((rank, rank), F32),
                pltpu.VMEM((rank, rank), F32),
                pltpu.SemaphoreType.DMA,
            ],
            compiler_params=pltpu.CompilerParams(vmem_limit_bytes=40 << 20),
        )(me, sketch_all, series_data, *summed)
    )


def solution(mesh):
    in_specs = (P(("groups", "series"), None), P(("groups", "series"), None))
    out_specs = (P(("groups", "series"), None), P(("groups", "series"), None))
    return jax.shard_map(body, mesh=mesh, in_specs=in_specs, out_specs=out_specs, check_vma=False)
```

```python
import functools
import math

import jax
import jax.numpy as jnp
from jax import lax
from jax.experimental import pallas as pl
from jax.experimental.pallas import tpu as pltpu
from jax.sharding import PartitionSpec as P

AXIS = "series"
EDGE = 256
HALF = 128
PIVOTS = 32
CHAINS = 2
F32 = jnp.float32
BF16 = jnp.bfloat16


def exchange(value, distance):
    n = lax.axis_size(AXIS)
    return lax.ppermute(value, AXIS, [(i, i ^ distance) for i in range(n)])


def piece(value, index, count):
    rows = value.shape[0] // count
    return lax.dynamic_slice_in_dim(value, index * rows, rows, 0)


def scatter_stage(value, low, count):
    me = (lax.axis_index(AXIS) >> low) & (count - 1)
    got = [exchange(piece(value, me ^ k, count), k << low) for k in range(1, count)]
    total = piece(value, me, count)
    for item in got:
        total = total + item
    return total


def gather_stage(value, low, count):
    me = (lax.axis_index(AXIS) >> low) & (count - 1)
    got = [value] + [exchange(value, k << low) for k in range(1, count)]
    if count == 2:
        return jnp.where(me == 0, jnp.concatenate(got), jnp.concatenate(got[::-1]))
    rows = value.shape[0]
    out = jnp.zeros((count * rows,) + value.shape[1:], value.dtype)
    for k in range(count):
        out = lax.dynamic_update_slice_in_dim(out, got[k], (me ^ k) * rows, 0)
    return out


def stages():
    n = lax.axis_size(AXIS)
    return [(0, 2), (1, 4), (3, n // 8)]


def tie(value, other):
    return lax.optimization_barrier((value, other))


def widen(rows, low, count):
    return jnp.concatenate([rows] + [exchange(rows, k << low) for k in range(1, count)])


def sum_everywhere(parts, rows):
    core, square, far = stages()
    parts = [scatter_stage(p, *core) for p in parts]
    parts[0], rows = tie(parts[0], rows)
    rows = widen(rows, *far)
    parts = [scatter_stage(p, *square) for p in parts]
    parts[1], rows = tie(parts[1], rows)
    parts = [scatter_stage(p, *far) for p in parts]
    rows = widen(rows, *square)
    parts = [gather_stage(p, *far) for p in parts]
    parts[1], rows = tie(parts[1], rows)
    rows = widen(rows, *core)
    parts = [gather_stage(p, *square) for p in parts]
    parts = [gather_stage(p, *core) for p in parts]
    return parts, rows


def layout(time_steps):
    nb = time_steps // EDGE
    off = [(i, j) for i in range(nb) for j in range(i)]
    chains = [[] for _ in range(CHAINS)]
    for k, ij in enumerate(off):
        chains[k * CHAINS // len(off)].append(ij)
    for i in range(nb):
        chains[i * CHAINS // nb].append((i, i))
    return chains


def chain_rows(chain):
    return sum(EDGE if i != j else EDGE * 3 // 4 for i, j in chain)


def three(value):
    high = value.astype(BF16)
    rest = value - high.astype(F32)
    mid = rest.astype(BF16)
    low = (rest - mid.astype(F32)).astype(BF16)
    return high, mid, low


def product(a, b, contract=((1,), (0,)), precision=None):
    return lax.dot_general(
        a, b, (contract, ((), ())), precision=precision, preferred_element_type=F32
    )


def moment_kernel(chains, a_ref, *out_refs):
    for chain, out in zip(chains, out_refs):
        row = 0
        for i, j in chain:
            left = a_ref[:, i * EDGE : (i + 1) * EDGE]
            block = product(left, a_ref[:, j * EDGE : (j + 1) * EDGE], ((0,), (0,)))
            if i != j:
                out[row : row + EDGE, :] = block
                row += EDGE
            else:
                cut = HALF + HALF // 2
                out[row : row + HALF, :HALF] = block[:HALF, :HALF]
                out[row : row + HALF, HALF:] = block[HALF:, HALF:]
                out[row + HALF : row + cut, :HALF] = block[HALF:cut, :HALF]
                out[row + HALF : row + cut, HALF:] = block[cut:, :HALF]
                row += EDGE * 3 // 4


def unpack(chains, refs, store):
    for chain, ref in zip(chains, refs):
        row = 0
        for i, j in chain:
            if i != j:
                block = ref[row : row + EDGE, :]
                row += EDGE
                store(i, j, block)
                store(j, i, block.T)
            else:
                first = ref[row : row + HALF, :HALF]
                last = ref[row : row + HALF, HALF:]
                tail = ref[row + HALF : row + HALF + HALF // 2, :]
                cross = jnp.concatenate([tail[:, :HALF], tail[:, HALF:]], axis=0)
                row += EDGE * 3 // 4
                store(
                    i,
                    i,
                    jnp.concatenate(
                        [
                            jnp.concatenate([first, cross.T], axis=1),
                            jnp.concatenate([cross, last], axis=1),
                        ],
                        axis=0,
                    ),
                )


def inverse_factor(x_ref, w_ref, beside=None):
    n = x_ref.shape[0]
    groups = PIVOTS // 8
    tiles = n // 128
    lane = lax.broadcasted_iota(jnp.int32, (8, 128), 1)
    sub = lax.broadcasted_iota(jnp.int32, (8, 128), 0)
    for k in range(n // PIVOTS):
        o = PIVOTS * k
        home, lo = o // 128, o % 128
        panel = [
            [x_ref[o + 8 * g : o + 8 * g + 8, 128 * t : 128 * t + 128] for t in range(tiles)]
            for g in range(groups)
        ]
        col = {
            (i, g): jnp.broadcast_to(panel[g][home][:, lo + i : lo + i + 1], (8, 128))
            for i in range(PIVOTS)
            for g in range(i // 8, groups)
        }
        in_block = (lane >= lo) & (lane < lo + PIVOTS)
        for g in range(groups):
            unit = jnp.where(lane - lo == sub + 8 * g, 1.0, 0.0)
            panel[g][home] = jnp.where(in_block, unit, panel[g][home])
        if beside is not None:
            beside(k)
        for j in range(PIVOTS):
            gj, s = j // 8, j % 8
            scale = lax.rsqrt(jnp.broadcast_to(col[j, gj][s : s + 1, :], (8, 128)))
            low = {g: col[j, g] * scale for g in range(gj, groups)}
            for i in range(j + 1, PIVOTS):
                other = jnp.broadcast_to(low[i // 8][i % 8 : i % 8 + 1, :], (8, 128))
                for g in range(i // 8, groups):
                    col[i, g] = col[i, g] - low[g] * other
            low[gj] = jnp.where(sub > s, low[gj], 0.0)
            for t in range(tiles):
                row = jnp.broadcast_to(panel[gj][t][s : s + 1, :], (8, 128)) * scale
                for g in range(gj, groups):
                    left = panel[g][t] - low[g] * row
                    panel[g][t] = jnp.where(sub == s, row, left) if g == gj else left
        for g in range(groups):
            for t in range(tiles):
                part = panel[g][t]
                if t > home:
                    part = jnp.zeros_like(part)
                elif t == home:
                    part = jnp.where(lane < lo + PIVOTS, part, 0.0)
                w_ref[o + 8 * g : o + 8 * g + 8, 128 * t : 128 * t + 128] = part
        nxt = o + PIVOTS
        if nxt < n:
            rows = jnp.concatenate([jnp.concatenate(p, axis=1) for p in panel], axis=0)
            first = nxt // 128 * 128
            a, b, c = three(rows)
            left = jnp.concatenate([a, a, a, b, b, c], axis=0)[:, first:]
            right = jnp.concatenate([a, b, c, a, b, a], axis=0)
            update = product(left, right, ((0,), (0,)))
            old = x_ref[nxt:, :]
            column = lax.broadcasted_iota(jnp.int32, old.shape, 1)
            old = jnp.where((column >= o) & (column < nxt), 0.0, old)
            x_ref[nxt:, :] = old - update[nxt - first :, :]


def finish_kernel(
    chains, rows_total, factor, me_ref, sketch_ref, a_hbm, *refs
):
    chain_refs, refs = refs[: len(chains)], refs[len(chains) :]
    range_ref, coef_ref, moment, a_ref, power, y_ref, back_ref, x_ref, w_ref, sem = refs
    time_steps, rank = sketch_ref.shape
    steps = coef_ref.shape[0]
    nb = time_steps // EDGE
    fetch = pltpu.make_async_copy(a_hbm, a_ref, sem)
    fetch.start()

    devices = time_steps // steps
    for k in range(devices):
        others = devices // 8
        away = k % others * 8 + k // others % 4 * 2 + k // others // 4
        block = sketch_ref[k * steps : (k + 1) * steps, :].astype(F32)
        spot = lax.bitwise_xor(me_ref[0], jnp.int32(away)) * steps
        y_ref[pl.ds(pl.multiple_of(spot, steps), steps), :] = block
    sketch_ref = back_ref
    sketch_ref[...] = y_ref[...].astype(BF16)

    def store(i, j, block):
        for p, part in enumerate(three(block)):
            moment[p, i * EDGE : (i + 1) * EDGE, j * EDGE : (j + 1) * EDGE] = part

    unpack(chains, chain_refs, store)

    def apply_moment(right_ref):
        for i in range(nb):
            band = slice(i * EDGE, (i + 1) * EDGE)
            total = product(moment[0, band, :], right_ref[...])
            total = total + product(moment[1, band, :], right_ref[...])
            y_ref[band, :] = total + product(moment[2, band, :], right_ref[...])

    def gram(left_ref):
        wide = product(left_ref[...], jnp.concatenate(three(y_ref[...]), axis=1), ((0,), (0,)))
        x_ref[...] = (wide[:, :rank] + wide[:, rank : 2 * rank] + wide[:, 2 * rank :]) / rows_total

    high = lax.Precision.HIGHEST
    apply_moment(sketch_ref)
    gram(sketch_ref)
    inverse_factor(x_ref, w_ref)
    for i in range(nb):
        band = slice(i * EDGE, (i + 1) * EDGE)
        back_ref[band, :] = (
            product(y_ref[band, :], w_ref[...], ((1,), (1,)), high) * factor
        ).astype(BF16)
    apply_moment(back_ref)
    gram(back_ref)
    fetch.wait()
    panels = rank // PIVOTS
    share = a_ref.shape[0] // panels

    def some_power(k):
        band = slice(k * share, (k + 1) * share)
        power[band, :] = product(a_ref[band, :], back_ref[...])

    inverse_factor(x_ref, w_ref, some_power)
    for k in range(panels):
        band = slice(k * share, (k + 1) * share)
        range_ref[band, :] = product(power[band, :], w_ref[...], ((1,), (1,)), high).astype(BF16)
    mine = y_ref[pl.ds(pl.multiple_of(me_ref[0] * steps, steps), steps), :]
    coef_ref[...] = (product(mine, w_ref[...], ((1,), (1,)), high) * factor).astype(BF16)


def body(series_data, sketch_matrix):
    devices_here = lax.axis_size(AXIS)
    local_rows = series_data.shape[0]
    rows_total = local_rows * devices_here
    local_steps, rank = sketch_matrix.shape
    time_steps = local_steps * devices_here
    factor = math.sqrt(time_steps) / rows_total
    chains = layout(time_steps)
    vmem = pl.BlockSpec(memory_space=pltpu.VMEM)

    partial = pl.pallas_call(
        functools.partial(moment_kernel, chains),
        out_shape=[jax.ShapeDtypeStruct((chain_rows(c), EDGE), F32) for c in chains],
        in_specs=[vmem],
        out_specs=[vmem] * len(chains),
        compiler_params=pltpu.CompilerParams(vmem_limit_bytes=20 << 20),
    )(series_data)
    summed, sketch_all = sum_everywhere(list(partial), sketch_matrix)
    me = lax.axis_index(AXIS).astype(jnp.int32).reshape(1)
    return tuple(
        pl.pallas_call(
            functools.partial(finish_kernel, chains, rows_total, factor),
            out_shape=[
                jax.ShapeDtypeStruct((local_rows, rank), BF16),
                jax.ShapeDtypeStruct((local_steps, rank), BF16),
            ],
            in_specs=[
                pl.BlockSpec(memory_space=pltpu.SMEM),
                vmem,
                pl.BlockSpec(memory_space=pltpu.HBM),
            ]
            + [vmem] * len(chains),
            out_specs=[vmem, vmem],
            scratch_shapes=[
                pltpu.VMEM((3, time_steps, time_steps), BF16),
                pltpu.VMEM(series_data.shape, BF16),
                pltpu.VMEM((local_rows, rank), F32),
                pltpu.VMEM((time_steps, rank), F32),
                pltpu.VMEM((time_steps, rank), BF16),
                pltpu.VMEM((rank, rank), F32),
                pltpu.VMEM((rank, rank), F32),
                pltpu.SemaphoreType.DMA,
            ],
            compiler_params=pltpu.CompilerParams(vmem_limit_bytes=40 << 20),
        )(me, sketch_all, series_data, *summed)
    )


def solution(mesh):
    in_specs = (P(("groups", "series"), None), P(("groups", "series"), None))
    out_specs = (P(("groups", "series"), None), P(("groups", "series"), None))
    return jax.shard_map(body, mesh=mesh, in_specs=in_specs, out_specs=out_specs, check_vma=False)
```

```python
import functools
import math

import jax
import jax.numpy as jnp
from jax import lax
from jax.experimental import pallas as pl
from jax.experimental.pallas import tpu as pltpu
from jax.sharding import PartitionSpec as P

AXIS = "series"
EDGE = 256
HALF = 128
PIVOTS = 32
CHAINS = 2
F32 = jnp.float32
BF16 = jnp.bfloat16


def exchange(value, distance):
    n = lax.axis_size(AXIS)
    return lax.ppermute(value, AXIS, [(i, i ^ distance) for i in range(n)])


def piece(value, index, count):
    rows = value.shape[0] // count
    return lax.dynamic_slice_in_dim(value, index * rows, rows, 0)


def scatter_stage(value, low, count):
    me = (lax.axis_index(AXIS) >> low) & (count - 1)
    got = [exchange(piece(value, me ^ k, count), k << low) for k in range(1, count)]
    total = piece(value, me, count)
    for item in got:
        total = total + item
    return total


def gather_stage(value, low, count):
    me = (lax.axis_index(AXIS) >> low) & (count - 1)
    got = [value] + [exchange(value, k << low) for k in range(1, count)]
    if count == 2:
        return jnp.where(me == 0, jnp.concatenate(got), jnp.concatenate(got[::-1]))
    rows = value.shape[0]
    out = jnp.zeros((count * rows,) + value.shape[1:], value.dtype)
    for k in range(count):
        out = lax.dynamic_update_slice_in_dim(out, got[k], (me ^ k) * rows, 0)
    return out


def stages():
    n = lax.axis_size(AXIS)
    return [(0, 2), (1, 4), (3, n // 8)]


def tie(value, other):
    return lax.optimization_barrier((value, other))


def widen(rows, low, count):
    return jnp.concatenate([rows] + [exchange(rows, k << low) for k in range(1, count)])


def sum_everywhere(parts, rows):
    core, square, far = stages()
    parts = [scatter_stage(p, *core) for p in parts]
    parts[0], rows = tie(parts[0], rows)
    rows = widen(rows, *far)
    parts = [scatter_stage(p, *square) for p in parts]
    parts[1], rows = tie(parts[1], rows)
    parts = [scatter_stage(p, *far) for p in parts]
    rows = widen(rows, *square)
    parts = [gather_stage(p, *far) for p in parts]
    parts[1], rows = tie(parts[1], rows)
    rows = widen(rows, *core)
    parts = [gather_stage(p, *square) for p in parts]
    parts = [gather_stage(p, *core) for p in parts]
    return parts, rows


def layout(time_steps):
    nb = time_steps // EDGE
    off = [(i, j) for i in range(nb) for j in range(i)]
    chains = [[] for _ in range(CHAINS)]
    for k, ij in enumerate(off):
        chains[k * CHAINS // len(off)].append(ij)
    for i in range(nb):
        chains[i * CHAINS // nb].append((i, i))
    return chains


def chain_rows(chain):
    return sum(EDGE if i != j else EDGE * 3 // 4 for i, j in chain)


def three(value):
    high = value.astype(BF16)
    rest = value - high.astype(F32)
    mid = rest.astype(BF16)
    low = (rest - mid.astype(F32)).astype(BF16)
    return high, mid, low


def product(a, b, contract=((1,), (0,)), precision=None):
    return lax.dot_general(
        a, b, (contract, ((), ())), precision=precision, preferred_element_type=F32
    )


def moment_kernel(chains, a_ref, *out_refs):
    for chain, out in zip(chains, out_refs):
        row = 0
        for i, j in chain:
            left = a_ref[:, i * EDGE : (i + 1) * EDGE]
            block = product(left, a_ref[:, j * EDGE : (j + 1) * EDGE], ((0,), (0,)))
            if i != j:
                out[row : row + EDGE, :] = block
                row += EDGE
            else:
                cut = HALF + HALF // 2
                out[row : row + HALF, :HALF] = block[:HALF, :HALF]
                out[row : row + HALF, HALF:] = block[HALF:, HALF:]
                out[row + HALF : row + cut, :HALF] = block[HALF:cut, :HALF]
                out[row + HALF : row + cut, HALF:] = block[cut:, :HALF]
                row += EDGE * 3 // 4


def unpack(chains, refs, store):
    for chain, ref in zip(chains, refs):
        row = 0
        for i, j in chain:
            if i != j:
                block = ref[row : row + EDGE, :]
                row += EDGE
                store(i, j, block)
                store(j, i, block.T)
            else:
                first = ref[row : row + HALF, :HALF]
                last = ref[row : row + HALF, HALF:]
                tail = ref[row + HALF : row + HALF + HALF // 2, :]
                cross = jnp.concatenate([tail[:, :HALF], tail[:, HALF:]], axis=0)
                row += EDGE * 3 // 4
                store(
                    i,
                    i,
                    jnp.concatenate(
                        [
                            jnp.concatenate([first, cross.T], axis=1),
                            jnp.concatenate([cross, last], axis=1),
                        ],
                        axis=0,
                    ),
                )


def inverse_factor(x_ref, w_ref, beside=None):
    n = x_ref.shape[0]
    groups = PIVOTS // 8
    tiles = n // 128
    lane = lax.broadcasted_iota(jnp.int32, (8, 128), 1)
    sub = lax.broadcasted_iota(jnp.int32, (8, 128), 0)
    for k in range(n // PIVOTS):
        o = PIVOTS * k
        home, lo = o // 128, o % 128
        panel = [
            [x_ref[o + 8 * g : o + 8 * g + 8, 128 * t : 128 * t + 128] for t in range(tiles)]
            for g in range(groups)
        ]
        col = {
            (i, g): jnp.broadcast_to(panel[g][home][:, lo + i : lo + i + 1], (8, 128))
            for i in range(PIVOTS)
            for g in range(i // 8, groups)
        }
        in_block = (lane >= lo) & (lane < lo + PIVOTS)
        for g in range(groups):
            unit = jnp.where(lane - lo == sub + 8 * g, 1.0, 0.0)
            panel[g][home] = jnp.where(in_block, unit, panel[g][home])
        if beside is not None:
            beside(k)
        for j in range(PIVOTS):
            gj, s = j // 8, j % 8
            scale = lax.rsqrt(jnp.broadcast_to(col[j, gj][s : s + 1, :], (8, 128)))
            low = {g: col[j, g] * scale for g in range(gj, groups)}
            for i in range(j + 1, PIVOTS):
                other = jnp.broadcast_to(low[i // 8][i % 8 : i % 8 + 1, :], (8, 128))
                for g in range(i // 8, groups):
                    col[i, g] = col[i, g] - low[g] * other
            low[gj] = jnp.where(sub > s, low[gj], 0.0)
            for t in range(tiles):
                row = jnp.broadcast_to(panel[gj][t][s : s + 1, :], (8, 128)) * scale
                for g in range(gj, groups):
                    left = panel[g][t] - low[g] * row
                    panel[g][t] = jnp.where(sub == s, row, left) if g == gj else left
        for g in range(groups):
            for t in range(tiles):
                part = panel[g][t]
                if t > home:
                    part = jnp.zeros_like(part)
                elif t == home:
                    part = jnp.where(lane < lo + PIVOTS, part, 0.0)
                w_ref[o + 8 * g : o + 8 * g + 8, 128 * t : 128 * t + 128] = part
        nxt = o + PIVOTS
        if nxt < n:
            rows = jnp.concatenate([jnp.concatenate(p, axis=1) for p in panel], axis=0)
            first = nxt // 128 * 128
            a, b, c = three(rows)
            left = jnp.concatenate([a, a, a, b, b, c], axis=0)[:, first:]
            right = jnp.concatenate([a, b, c, a, b, a], axis=0)
            update = product(left, right, ((0,), (0,)))
            old = x_ref[nxt:, :]
            column = lax.broadcasted_iota(jnp.int32, old.shape, 1)
            old = jnp.where((column >= o) & (column < nxt), 0.0, old)
            x_ref[nxt:, :] = old - update[nxt - first :, :]


def finish_kernel(
    chains, rows_total, factor, me_ref, sketch_ref, a_hbm, *refs
):
    chain_refs, refs = refs[: len(chains)], refs[len(chains) :]
    range_ref, coef_ref, moment, a_ref, power, y_ref, back_ref, x_ref, w_ref, sem = refs
    time_steps, rank = sketch_ref.shape
    steps = coef_ref.shape[0]
    nb = time_steps // EDGE
    fetch = pltpu.make_async_copy(a_hbm, a_ref, sem)
    fetch.start()

    devices = time_steps // steps
    for k in range(devices):
        others = devices // 8
        away = k % others * 8 + k // others % 4 * 2 + k // others // 4
        block = sketch_ref[k * steps : (k + 1) * steps, :].astype(F32)
        spot = lax.bitwise_xor(me_ref[0], jnp.int32(away)) * steps
        y_ref[pl.ds(pl.multiple_of(spot, steps), steps), :] = block
    sketch_ref = back_ref
    sketch_ref[...] = y_ref[...].astype(BF16)

    def store(i, j, block):
        for p, part in enumerate(three(block)):
            moment[p, i * EDGE : (i + 1) * EDGE, j * EDGE : (j + 1) * EDGE] = part

    unpack(chains, chain_refs, store)

    def apply_moment(right_ref):
        for i in range(nb):
            band = slice(i * EDGE, (i + 1) * EDGE)
            total = product(moment[0, band, :], right_ref[...])
            total = total + product(moment[1, band, :], right_ref[...])
            y_ref[band, :] = total + product(moment[2, band, :], right_ref[...])

    def gram(left_ref):
        wide = product(left_ref[...], jnp.concatenate(three(y_ref[...]), axis=1), ((0,), (0,)))
        x_ref[...] = (wide[:, :rank] + wide[:, rank : 2 * rank] + wide[:, 2 * rank :]) / rows_total

    high = lax.Precision.HIGHEST
    apply_moment(sketch_ref)
    gram(sketch_ref)
    inverse_factor(x_ref, w_ref)
    half = time_steps // 2
    for i in range(2):
        band = slice(i * half, (i + 1) * half)
        back_ref[band, :] = (
            product(y_ref[band, :], w_ref[...], ((1,), (1,)), high) * factor
        ).astype(BF16)
    apply_moment(back_ref)
    gram(back_ref)
    fetch.wait()
    panels = rank // PIVOTS
    share = a_ref.shape[0] // panels

    def some_power(k):
        band = slice(k * share, (k + 1) * share)
        power[band, :] = product(a_ref[band, :], back_ref[...])

    inverse_factor(x_ref, w_ref, some_power)
    half = a_ref.shape[0] // 2
    for k in range(2):
        band = slice(k * half, (k + 1) * half)
        range_ref[band, :] = product(power[band, :], w_ref[...], ((1,), (1,)), high).astype(BF16)
    mine = y_ref[pl.ds(pl.multiple_of(me_ref[0] * steps, steps), steps), :]
    coef_ref[...] = (product(mine, w_ref[...], ((1,), (1,)), high) * factor).astype(BF16)


def body(series_data, sketch_matrix):
    devices_here = lax.axis_size(AXIS)
    local_rows = series_data.shape[0]
    rows_total = local_rows * devices_here
    local_steps, rank = sketch_matrix.shape
    time_steps = local_steps * devices_here
    factor = math.sqrt(time_steps) / rows_total
    chains = layout(time_steps)
    vmem = pl.BlockSpec(memory_space=pltpu.VMEM)

    partial = pl.pallas_call(
        functools.partial(moment_kernel, chains),
        out_shape=[jax.ShapeDtypeStruct((chain_rows(c), EDGE), F32) for c in chains],
        in_specs=[vmem],
        out_specs=[vmem] * len(chains),
        compiler_params=pltpu.CompilerParams(vmem_limit_bytes=20 << 20),
    )(series_data)
    summed, sketch_all = sum_everywhere(list(partial), sketch_matrix)
    me = lax.axis_index(AXIS).astype(jnp.int32).reshape(1)
    return tuple(
        pl.pallas_call(
            functools.partial(finish_kernel, chains, rows_total, factor),
            out_shape=[
                jax.ShapeDtypeStruct((local_rows, rank), BF16),
                jax.ShapeDtypeStruct((local_steps, rank), BF16),
            ],
            in_specs=[
                pl.BlockSpec(memory_space=pltpu.SMEM),
                vmem,
                pl.BlockSpec(memory_space=pltpu.HBM),
            ]
            + [vmem] * len(chains),
            out_specs=[vmem, vmem],
            scratch_shapes=[
                pltpu.VMEM((3, time_steps, time_steps), BF16),
                pltpu.VMEM(series_data.shape, BF16),
                pltpu.VMEM((local_rows, rank), F32),
                pltpu.VMEM((time_steps, rank), F32),
                pltpu.VMEM((time_steps, rank), BF16),
                pltpu.VMEM((rank, rank), F32),
                pltpu.VMEM((rank, rank), F32),
                pltpu.SemaphoreType.DMA,
            ],
            compiler_params=pltpu.CompilerParams(vmem_limit_bytes=40 << 20),
        )(me, sketch_all, series_data, *summed)
    )


def solution(mesh):
    in_specs = (P(("groups", "series"), None), P(("groups", "series"), None))
    out_specs = (P(("groups", "series"), None), P(("groups", "series"), None))
    return jax.shard_map(body, mesh=mesh, in_specs=in_specs, out_specs=out_specs, check_vma=False)
```
